32 devices in a mesh: seq: 8 (over y, x, core), emb: 4 (over z).
Axes of the slice: x: 2, y: 2, z: 4, core: 2. Of those that a mesh axis runs over, the one named last changes fastest.
Arguments:
- source: bfloat16 [8192, 1024], P('seq', 'emb'), may hold values from -6 to 6
- target: bfloat16 [8192, 1024], P('seq', 'emb'), may hold values from -6 to 6
- doc_ids: int32 [8192], replicated, may hold values from 0 to 127, never falling along the last dimension, each value on 1 to 512 neighbouring positions
- offsets: int32 [128], P(('seq', 'emb')), may hold values from -2048 to 2048, as said below
Outputs:
- projected: bfloat16 [8192, 1024], P('seq', 'emb')
- row_mass: float32 [8192], P(('seq', 'emb'))
The draws below stay inside these ranges and needn't reach their ends.
Inputs may be any that keep to these rules, and one draw needn't show every extreme that they name: doc_ids never fall along the sentences. `offsets`: both ends of the range occur in every draw.
All inputs are finite; a program needn't handle non-finite values.
Results may differ from the reference program's by a relative error of at most 0.006.
Values may be sent and summed in bfloat16 or wider, within the bound.
A program may use at most 128 MiB of HBM per device.

```python
import math
import jax
import jax.numpy as jnp
import numpy as np
from jax import lax

D = 1024
ROWS_DEV = 256
BAND = 2048
OFFSET_BLOCK = 64
ITERS = 3
SENTENCES = 8192
DOCS = 128


def draw_offsets(key, part):
    count = SENTENCES // OFFSET_BLOCK
    base = jax.random.randint(jax.random.fold_in(key, 11), (count,), -BAND, BAND + 1, dtype=jnp.int32)
    picks = jax.random.permutation(jax.random.fold_in(key, 12), count)
    base = base.at[picks[0]].set(BAND)
    base = base.at[picks[1]].set(-BAND)
    return base.astype(jnp.int32)


def steps_of(key, dims, split, smallest, top_value):
    def one(axis_at, shards_of):
        heights = jax.random.uniform(jax.random.fold_in(jax.random.fold_in(key, 6), axis_at), (shards_of,), jnp.float32, smallest / len(split), top_value / len(split))
        return jnp.repeat(jnp.exp(heights), dims[axis_at] // shards_of).reshape((-1,) + (1,) * (len(dims) - axis_at - 1))

    gain = one(*split[0])
    for cut in split[1:]:
        gain = gain * one(*cut)
    return gain


def profile(count, total, most, skew):
    loads = [(1 << 20) // math.isqrt(standing ** skew) + 1 for standing in range(2, count + 1)]
    spare, holding = total - most - (count - 1), [1] * (count - 1)
    while spare > 0:
        free = [i for i in range(count - 1) if holding[i] < most]
        mass, budget = sum([loads[i] for i in free]), spare
        for i in free:
            addition = min(most - holding[i], max(1, budget * loads[i] // mass), spare)
            holding[i] = holding[i] + addition
            spare = spare - addition
    return np.array([most] + holding)


def uneven_parts(stream_key, number_of, total, bound, slope):
    if number_of == 2:
        one = jax.random.randint(stream_key, (), max(1, total - bound), min(bound, total - 1) + 1)
        return jnp.stack([one, total - one])
    lengths = jnp.asarray(profile(number_of, total, bound, slope), jnp.int32)
    pairs = (number_of - 1) // 2
    donor, receiver = lengths[1:1 + 2 * pairs:2], lengths[2:2 + 2 * pairs:2]
    slack = jnp.minimum(donor - 1, bound - receiver)
    passed = jax.random.randint(jax.random.fold_in(stream_key, 1), (pairs,), 0, 1 << 20) % (slack + 1)
    lengths = lengths.at[1:1 + 2 * pairs:2].set(donor - passed).at[2:2 + 2 * pairs:2].set(receiver + passed)
    return lengths[jax.random.permutation(jax.random.fold_in(stream_key, 2), number_of)]


def gaussian(rng, shape, deviation, most, pieces=(), held_as=jnp.bfloat16):
    result = deviation * jax.random.normal(rng, shape, jnp.float32)
    if pieces:
        result = result * steps_of(rng, shape, pieces, -0.22, 0.18)
    return jnp.clip(result, -most, most).astype(held_as)


def setup_inputs(seed: int = 0) -> dict:
    streams_of = jax.random.split(jax.random.key(seed), 5)
    return {
        "source": gaussian(streams_of[0], (SENTENCES, D), 1.0, 6.0, ((0, 8), (1, 4))),
        "target": gaussian(streams_of[1], (SENTENCES, D), 1.0, 6.0, ((0, 8), (1, 4))),
        "doc_ids": jnp.searchsorted(jnp.cumsum(uneven_parts(streams_of[2], DOCS, SENTENCES, min(512, SENTENCES // 2), 0)), jnp.arange(SENTENCES), side="right").astype(jnp.int32),
        "offsets": draw_offsets(jax.random.fold_in(streams_of[4], 71), 0),
    }


INV_EPS = 50.0
PENALTY = 0.04

def kernel_blocks(source, target, doc_ids, offsets):
    reach = 2 * BAND
    width = ROWS_DEV + 2 * reach
    blocks = SENTENCES // ROWS_DEV
    src_scale = lax.rsqrt(lax.optimization_barrier(jnp.sum(jnp.square(source.astype(jnp.float32)), axis=1)) + 1e-06)
    tgt_scale = lax.rsqrt(lax.optimization_barrier(jnp.sum(jnp.square(target.astype(jnp.float32)), axis=1)) + 1e-06)
    pad_target = jnp.pad(target, ((reach, reach), (0, 0)))
    pad_scale = jnp.pad(tgt_scale, (reach, reach))
    pad_docs = jnp.pad(doc_ids, (reach, reach), constant_values=-1)
    row_offsets = jnp.repeat(offsets, OFFSET_BLOCK)

    def one_block(index):
        start = (index * ROWS_DEV).astype(jnp.int32)
        rows = lax.dynamic_slice_in_dim(source, start, ROWS_DEV, 0)
        window = lax.dynamic_slice_in_dim(pad_target, start, width, 0)
        dots = lax.dot_general(rows, window, (((1,), (1,)), ((), ())), preferred_element_type=jnp.float32)
        cosine = dots * lax.dynamic_slice_in_dim(src_scale, start, ROWS_DEV, 0)[:, None] * lax.dynamic_slice_in_dim(pad_scale, start, width, 0)[None, :]
        src_pos = start + jnp.arange(ROWS_DEV, dtype=jnp.int32)
        tgt_pos = start - reach + jnp.arange(width, dtype=jnp.int32)
        shifted = lax.dynamic_slice_in_dim(row_offsets, start, ROWS_DEV, 0)
        band = (jnp.abs(tgt_pos[None, :] - src_pos[:, None] - shifted[:, None]) <= BAND) & (tgt_pos[None, :] >= 0) & (tgt_pos[None, :] < SENTENCES)
        same = lax.dynamic_slice_in_dim(doc_ids, start, ROWS_DEV, 0)[:, None] == lax.dynamic_slice_in_dim(pad_docs, start, width, 0)[None, :]
        logits = (cosine - jnp.where(same, 0.0, PENALTY)) * INV_EPS
        return jnp.where(band, jnp.exp(logits), 0.0).astype(jnp.float32)
    return lax.map(one_block, jnp.arange(blocks, dtype=jnp.int32))

def reference(source, target, doc_ids, offsets):
    reach = 2 * BAND
    width = ROWS_DEV + 2 * reach
    blocks = SENTENCES // ROWS_DEV
    kernels = kernel_blocks(source, target, doc_ids, offsets)
    starts = jnp.arange(blocks, dtype=jnp.int32) * ROWS_DEV
    pad_scaling = jnp.pad(jnp.ones((SENTENCES,), jnp.float32), (reach, reach))

    def row_sums(scaling):

        def one_row(item):
            kern, start = item
            return lax.optimization_barrier(jnp.sum(kern * lax.dynamic_slice_in_dim(scaling, start, width, 0)[None, :], axis=1))
        return lax.map(one_row, (kernels, starts))

    def add_cols(carry, item):
        kern, weight, start = item
        part = lax.optimization_barrier(jnp.sum(kern * weight[:, None], axis=0))
        current = lax.dynamic_slice_in_dim(carry, start, width, 0)
        return (lax.dynamic_update_slice_in_dim(carry, current + part, start, 0), None)
    inverse = jnp.zeros((blocks, ROWS_DEV), jnp.float32)
    for step in range(ITERS):
        inverse = 1.0 / row_sums(pad_scaling)
        columns, _ = lax.scan(add_cols, jnp.zeros((SENTENCES + 2 * reach,), jnp.float32), (kernels, inverse, starts))
        pad_scaling = jnp.pad(1.0 / columns[reach:reach + SENTENCES], (reach, reach))
    final = row_sums(pad_scaling)
    row_mass = (inverse * final).reshape(SENTENCES)
    pad_target = jnp.pad(target, ((reach, reach), (0, 0)))

    def mix(item):
        kern, totals, start = item
        weights = (kern * lax.dynamic_slice_in_dim(pad_scaling, start, width, 0)[None, :] / totals[:, None]).astype(jnp.bfloat16)
        window = lax.dynamic_slice_in_dim(pad_target, start, width, 0)
        return jnp.dot(weights, window, preferred_element_type=jnp.float32).astype(jnp.bfloat16)
    projected = lax.map(mix, (kernels, final, starts)).reshape(SENTENCES, D)
    return (projected, row_mass)
```

```python
import functools

import jax
import jax.numpy as jnp
from jax import lax
from jax.experimental import pallas as pl
from jax.experimental.pallas import tpu as pltpu
from jax.sharding import PartitionSpec as P

BAND = 2048
OFFSET_BLOCK = 64
ITERS = 3


INV_EPS = 50.0
PENALTY = 0.04


def shifted_2(block, axis, distance):
    devices = range(lax.axis_size(axis))
    route = [(i - distance, i) for i in devices if i - distance in devices]
    return lax.ppermute(block, axis, route)


def per_device(source, target, doc_ids, offsets):
    n_emb = lax.axis_size("emb")
    rows_dev = source.shape[0] // n_emb
    place = lax.axis_index(("seq", "emb"))
    sentences = doc_ids.shape[0]
    reach = 2 * BAND
    hops = reach // rows_dev
    width = rows_dev + 2 * reach
    src_rows, tgt_rows = (
        lax.all_to_all(source, "emb", split_axis=0, concat_axis=1, tiled=True),
        lax.all_to_all(target, "emb", split_axis=0, concat_axis=1, tiled=True),
    )
    lower = {}
    upper = {}
    for dist in range(1, hops + 1):
        for sign in (1, -1):
            moved = shifted_2(tgt_rows, ("seq", "emb"), -sign * dist)
            if sign > 0:
                upper[dist] = moved
            else:
                lower[dist] = moved
    pieces = (
        [lower[dist] for dist in range(hops, 0, -1)]
        + [tgt_rows]
        + [upper[dist] for dist in range(1, hops + 1)]
    )
    window = jnp.concatenate(pieces, axis=0)
    src_scale = lax.rsqrt(jnp.sum(jnp.square(src_rows.astype(jnp.float32)), axis=1) + 1e-06)
    tgt_scale = lax.rsqrt(jnp.sum(jnp.square(window.astype(jnp.float32)), axis=1) + 1e-06)
    first_row = place * rows_dev
    src_pos = first_row + jnp.arange(rows_dev, dtype=jnp.int32)
    tgt_pos = first_row - reach + jnp.arange(width, dtype=jnp.int32)
    valid = (tgt_pos >= 0) & (tgt_pos < sentences)
    shifted = jnp.repeat(offsets, OFFSET_BLOCK)
    band = (jnp.abs(tgt_pos[None, :] - src_pos[:, None] - shifted[:, None]) <= BAND) & valid[
        None, :
    ]
    pad_docs = jnp.pad(doc_ids, (reach, reach), constant_values=-1)
    same = (
        lax.dynamic_slice_in_dim(doc_ids, first_row, rows_dev, 0)[:, None]
        == lax.dynamic_slice_in_dim(pad_docs, first_row, width, 0)[None, :]
    )
    penalty = jnp.where(same, 0.0, PENALTY)

    def cosines():
        dots = lax.dot_general(
            src_rows, window, (((1,), (1,)), ((), ())), preferred_element_type=jnp.float32
        )
        return dots * src_scale[:, None] * tgt_scale[None, :]

    def to_kernel(cosine):
        return jnp.where(band, jnp.exp((cosine - penalty) * INV_EPS), 0.0)

    def kernel():
        return to_kernel(cosines())

    scaling = valid.astype(jnp.float32)
    inverse = jnp.zeros((rows_dev,), jnp.float32)
    for step in range(ITERS):
        kern = kernel()
        inverse = 1.0 / jnp.sum(kern * scaling[None, :], axis=1)
        part = jnp.sum(kern * inverse[:, None], axis=0)
        owned = part[reach : reach + rows_dev]
        for lag in range(-hops, hops + 1):
            if lag != 0:
                begin = reach + lag * rows_dev
                owned = owned + shifted_2(part[begin : begin + rows_dev], ("seq", "emb"), lag)
        own_scaling = 1.0 / owned
        parts_list = []
        for lag in range(-hops, hops + 1):
            if lag == 0:
                parts_list.append(own_scaling)
            else:
                parts_list.append(shifted_2(own_scaling, ("seq", "emb"), -lag))
        scaling = jnp.concatenate(parts_list, axis=0)
    kern = kernel()
    totals = jnp.sum(kern * scaling[None, :], axis=1)
    row_mass = inverse * totals
    weights = (kern * scaling[None, :] / totals[:, None]).astype(jnp.bfloat16)
    mixed = jnp.dot(weights, window, preferred_element_type=jnp.float32).astype(jnp.bfloat16)
    projected = lax.all_to_all(mixed, "emb", split_axis=1, concat_axis=0, tiled=True)
    return (projected, row_mass)


F32 = jnp.float32
BF16 = jnp.bfloat16
MESH = pl.DeviceIdType.MESH


def flip(value, mask):
    for bit in (1, 2, 4):
        if mask & bit:
            value = value + bit * (1 - 2 * ((value // bit) % 2))
    return value


def fused_kernel(
    src_in, tgt_in, offs_in, sdoc, tdoc, out, mass,
    src_all, tgt_all, offs, kmat, wmat, sscale, tscale, rowacc, rowbuf, invcol, invrow, scal, colpart,
    colbuf, piece, pieces_in, z_ssem, z_rsem, t_ssem, t_rsem, row_ssem, row_rsem, col_ssem, col_rsem,
    p_ssem, p_rsem,
):
    n_seq, n_emb = lax.axis_size("seq"), lax.axis_size("emb")
    s, e = lax.axis_index("seq"), lax.axis_index("emb")
    eh, el = e // 2, e % 2
    block, feats = src_in.shape
    rows = src_all.shape[0]
    held = block // 2
    half = held // 2

    def remote(src, dst, ssem, rsem, seq, emb):
        return pltpu.make_async_remote_copy(
            src_ref=src, dst_ref=dst, send_sem=ssem, recv_sem=rsem,
            device_id=(seq, emb), device_id_type=MESH,
        )

    barrier = pltpu.get_barrier_semaphore()
    for j in range(1, n_emb):
        pl.semaphore_signal(barrier, inc=1, device_id=(s, flip(e, j)), device_id_type=MESH)
    for k in range(1, n_seq):
        pl.semaphore_signal(barrier, inc=1, device_id=(flip(s, k), e), device_id_type=MESH)
        pl.semaphore_signal(barrier, inc=1, device_id=(flip(s, k), flip(e, 2)), device_id_type=MESH)
    pl.semaphore_wait(barrier, n_emb - 1 + 2 * (n_seq - 1))

    def cols(f):
        return pl.ds(pl.multiple_of(f * feats, feats), feats)

    def region(slot, j, start=0, count=held):
        return tgt_all.at[pl.ds(pl.multiple_of(slot * held + start, half), count), cols(flip(e, j))]

    sent = []

    def start(copy):
        copy.start()
        sent.append(copy)

    mine_t = pl.ds(pl.multiple_of(s * held, held), held)
    for j in range(1, n_emb):
        peer = flip(e, j)
        start(remote(
            tgt_in.at[pl.ds(pl.multiple_of((peer % 2) * held, held), held), :],
            tgt_all.at[mine_t, cols(e)], z_ssem.at[0, j], z_rsem.at[0, j], s, peer,
        ))
    start(remote(offs_in, offs.at[el], z_ssem.at[2, 0], z_rsem.at[2, 0], s, flip(e, 1)))
    for j in range(1, n_emb):
        peer = flip(e, j)
        start(remote(
            src_in.at[pl.ds(pl.multiple_of((peer // 2) * rows, rows), rows), :],
            src_all.at[:, cols(e)], z_ssem.at[1, j], z_rsem.at[1, j], s, peer,
        ))
    tgt_all[mine_t, cols(e)] = tgt_in[pl.ds(pl.multiple_of(el * held, held), held), :]
    src_all[:, cols(e)] = src_in[pl.ds(pl.multiple_of(eh * rows, rows), rows), :]
    offs[el] = offs_in[...]

    count = [0]

    def send(slot, j, k, to, begin=0, length=held, part=0):
        at = region(slot, j, begin, length)
        start(remote(at, at, t_ssem.at[count[0]], t_rsem.at[k, j, part], flip(s, to), e))
        count[0] += 1

    def arrived(k, j, begin=0, length=held, part=0):
        at = region(flip(s, k), j, begin, length)
        remote(at, at, t_ssem.at[0], t_rsem.at[k, j, part], s, e).wait_recv()

    def first(j):
        if j:
            at = region(s, j)
            remote(at, at, z_ssem.at[0, 0], z_rsem.at[0, j], s, e).wait_recv()
        send(s, j, 2, 2)
        send(s, j, 4, 4)
        send(s, j, 1, 1)

    def second(j):
        arrived(2, j)
        send(flip(s, 2), j, 6, 4, 0, half, 0)
        send(flip(s, 2), j, 3, 1)
        arrived(4, j)
        send(flip(s, 4), j, 6, 2, half, half, 1)
        send(flip(s, 4), j, 5, 1)

    def third(j):
        for part in range(2):
            arrived(6, j, part * half, half, part)
            send(flip(s, 6), j, 7, 1, part * half, half, part)

    for step in range(n_emb + 2):
        for stage, lag in ((first, 0), (second, 1), (third, 2)):
            if 0 <= step - lag < n_emb:
                stage(step - lag)

    for j in range(1, n_emb):
        at = src_all.at[:, cols(flip(e, j))]
        remote(at, at, z_ssem.at[1, 0], z_rsem.at[1, j], s, e).wait_recv()
    at = offs.at[1 - el]
    remote(at, at, z_ssem.at[2, 0], z_rsem.at[2, 0], s, e).wait_recv()

    lanes = 128
    depth = src_all.shape[1]

    @pl.loop(0, rows // 64)
    def _(r):
        at = pl.ds(pl.multiple_of(r * 64, 64), 64)
        acc = jnp.zeros((64, lanes), F32)
        for c in range(depth // lanes):
            x = src_all[at, pl.ds(c * lanes, lanes)].astype(F32)
            acc = acc + x * x
        total = jnp.sum(acc, axis=1, keepdims=True)
        sscale[at, :] = jnp.broadcast_to(lax.rsqrt(total + 1e-6), (64, lanes))

    for j in range(n_emb):
        for k in (1, 3, 5):
            arrived(k, j)
        for part in range(2):
            arrived(7, j, part * half, half, part)

    @pl.loop(0, n_seq)
    def _(slot):
        base = slot * held
        at = pl.ds(pl.multiple_of(base, held), held)

        @pl.loop(0, rows // 256)
        def _(r):
            rt = pl.ds(pl.multiple_of(r * 256, 256), 256)
            kmat[rt, at] = lax.dot_general(
                src_all[rt, :], tgt_all[at, :], (((1,), (1,)), ((), ())),
                preferred_element_type=F32,
            )

        @pl.loop(0, held // lanes)
        def _(c):
            tt = pl.ds(pl.multiple_of(base + c * lanes, lanes), lanes)
            acc = jnp.zeros((lanes, lanes), F32)
            for d in range(depth // lanes):
                x = tgt_all[tt, pl.ds(d * lanes, lanes)].astype(F32)
                acc = acc + x * x
            total = jnp.sum(jnp.transpose(acc), axis=0, keepdims=True)
            tscale[slot, :, pl.ds(pl.multiple_of(c * lanes, lanes), lanes)] = jnp.broadcast_to(
                lax.rsqrt(total + 1e-6), (8, lanes)
            )

    per_part = offs_in.shape[0]

    @pl.loop(0, rows // OFFSET_BLOCK)
    def _(r):
        at = pl.ds(pl.multiple_of(r * OFFSET_BLOCK, OFFSET_BLOCK), OFFSET_BLOCK)
        shift = offs[r // per_part, r % per_part, 0:1, :]
        pos = (
            s * block + eh * rows + r * OFFSET_BLOCK
            + lax.broadcasted_iota(jnp.int32, (OFFSET_BLOCK, lanes), 0) + shift
        )
        docs = sdoc[at, :]
        scale = sscale[at, :]
        acc = jnp.zeros((OFFSET_BLOCK, lanes), F32)

        def one(slot, acc):
            for c in range(held // lanes):
                ct = pl.ds(pl.multiple_of(slot * held + c * lanes, lanes), lanes)
                cl = pl.ds(c * lanes, lanes)
                tpos = (
                    slot * block + el * held + c * lanes
                    + lax.broadcasted_iota(jnp.int32, (1, lanes), 1)
                )
                cosine = kmat[at, ct] * scale * tscale[slot, 0:1, cl]
                penalty = jnp.where(docs == tdoc[slot, 0:1, cl], 0.0, PENALTY)
                value = jnp.exp((cosine - penalty) * INV_EPS)
                value = jnp.where(jnp.abs(tpos - pos) <= BAND, value, 0.0)
                kmat[at, ct] = value
                acc = acc + value
            return acc

        rowacc[at, :] = lax.fori_loop(0, n_seq, one, acc)

    def row_exchange(step):
        turned = jnp.transpose(rowacc[...])
        part = turned[0:8]
        for g in range(1, lanes // 8):
            part = part + turned[8 * g : 8 * g + 8]
        rowbuf[step, 0] = part
        copy = remote(
            rowbuf.at[step, 0], rowbuf.at[step, 1], row_ssem.at[step], row_rsem.at[step],
            s, flip(e, 1),
        )
        copy.start()
        copy.wait()
        return jnp.sum(part + rowbuf[step, 1], axis=0, keepdims=True)

    index = s * 2 + eh
    peers = 2 * n_seq

    @pl.loop(0, ITERS)
    def _(step):
        inverse = 1.0 / row_exchange(step)
        invrow[...] = jnp.broadcast_to(inverse, invrow.shape)
        invcol[...] = jnp.transpose(jnp.broadcast_to(inverse, (lanes, rows)))

        @pl.loop(0, n_seq)
        def _(slot):
            for c in range(held // lanes):
                ct = pl.ds(pl.multiple_of(slot * held + c * lanes, lanes), lanes)
                colpart[slot, :, pl.ds(c * lanes, lanes)] = jnp.sum(
                    (kmat[:, ct] * invcol[...]).reshape(rows // 8, 8, lanes), axis=0
                )

        for slot in range(n_seq):
            colbuf[step, index, slot : slot + 1, :] = jnp.sum(colpart[slot], axis=0, keepdims=True)

        def col_copy(p):
            to = (index + p) % peers
            return remote(
                colbuf.at[step, index], colbuf.at[step, index],
                col_ssem.at[step, p], col_rsem.at[step, p], to // 2, (to % 2) * 2 + el,
            )

        @pl.loop(1, peers)
        def _(p):
            col_copy(p).start()

        @pl.loop(1, peers)
        def _(p):
            owner = (index + peers - p) % peers
            at = colbuf.at[step, owner]
            remote(at, at, col_ssem.at[step, 0], col_rsem.at[step, p], s, e).wait_recv()

        total = colbuf[step, 0]
        for p in range(1, peers):
            total = total + colbuf[step, p]
        scal[...] = 1.0 / total

        @pl.loop(1, peers)
        def _(p):
            col_copy(p).wait_send()

        @pl.loop(0, rows // 64)
        def _(r):
            at = pl.ds(pl.multiple_of(r * 64, 64), 64)
            acc = jnp.zeros((64, lanes), F32)
            for slot in range(n_seq):
                for c in range(held // lanes):
                    acc = acc + kmat[at, pl.ds(slot * held + c * lanes, lanes)] * (
                        scal[slot : slot + 1, c * lanes : (c + 1) * lanes]
                    )
            rowacc[at, :] = acc

    totals = row_exchange(ITERS)
    mass[...] = invrow[...] * totals
    invcol[...] = jnp.transpose(jnp.broadcast_to(1.0 / totals, (lanes, rows)))

    @pl.loop(0, rows // 64)
    def _(r):
        at = pl.ds(pl.multiple_of(r * 64, 64), 64)
        inv = invcol[at, :]
        for slot in range(n_seq):
            for c in range(held // lanes):
                ct = pl.ds(slot * held + c * lanes, lanes)
                wmat[at, ct] = (
                    kmat[at, ct] * scal[slot : slot + 1, c * lanes : (c + 1) * lanes] * inv
                ).astype(BF16)

    copies = []
    for j in (1, 2, 3, 0):
        f = flip(e, j)

        @pl.loop(0, rows // 256)
        def _(r):
            rt = pl.ds(pl.multiple_of(r * 256, 256), 256)
            piece[j, rt, :] = jnp.dot(
                wmat[rt, :], tgt_all[:, cols(f)], preferred_element_type=F32
            ).astype(BF16)

        if j:
            copy = remote(piece.at[j], pieces_in.at[j], p_ssem.at[j], p_rsem.at[j], s, f)
            copy.start()
            copies.append(copy)
    for copy in copies:
        copy.wait_recv()
    mine = pl.ds(pl.multiple_of(eh * rows, rows), rows)
    other = pl.ds(pl.multiple_of((1 - eh) * rows, rows), rows)
    out[mine, :] = (piece[0].astype(F32) + pieces_in[1].astype(F32)).astype(BF16)
    out[other, :] = (pieces_in[2].astype(F32) + pieces_in[3].astype(F32)).astype(BF16)
    for copy in copies + sent:
        copy.wait_send()


def fused_device(source, target, doc_ids, offsets):
    n_seq, n_emb = lax.axis_size("seq"), lax.axis_size("emb")
    s, e = lax.axis_index("seq"), lax.axis_index("emb")
    block, feats = source.shape
    held = rows = block // 2
    depth = feats * n_emb
    width = n_seq * held
    tdoc = lax.dynamic_index_in_dim(doc_ids.reshape(n_seq, 2, held), e % 2, 1, keepdims=False)
    sdoc = lax.dynamic_slice_in_dim(doc_ids, s * block + (e // 2) * rows, rows, 0)
    sdoc = jnp.broadcast_to(sdoc[:, None], (rows, 128))
    tdoc = jnp.broadcast_to(tdoc[:, None], (n_seq, 8, held))
    offs = jnp.broadcast_to(offsets[:, None, None], (offsets.shape[0], 8, 128))
    vmem = pl.BlockSpec(memory_space=pltpu.VMEM)
    dma = pltpu.SemaphoreType.DMA
    projected, mass = pl.pallas_call(
        fused_kernel,
        out_shape=(
            jax.ShapeDtypeStruct((block, feats), BF16),
            jax.ShapeDtypeStruct((8, rows), F32),
        ),
        in_specs=[vmem] * 5,
        out_specs=(vmem, vmem),
        scratch_shapes=[
            pltpu.VMEM((rows, depth), BF16),
            pltpu.VMEM((width, depth), BF16),
            pltpu.VMEM((2, offsets.shape[0], 8, 128), jnp.int32),
            pltpu.VMEM((rows, width), F32),
            pltpu.VMEM((rows, width), BF16),
            pltpu.VMEM((rows, 128), F32),
            pltpu.VMEM((n_seq, 8, held), F32),
            pltpu.VMEM((rows, 128), F32),
            pltpu.VMEM((ITERS + 1, 2, 8, rows), F32),
            pltpu.VMEM((rows, 128), F32),
            pltpu.VMEM((8, rows), F32),
            pltpu.VMEM((n_seq, held), F32),
            pltpu.VMEM((n_seq, 8, held), F32),
            pltpu.VMEM((ITERS, 2 * n_seq, n_seq, held), F32),
            pltpu.VMEM((n_emb, rows, feats), BF16),
            pltpu.VMEM((n_emb, rows, feats), BF16),
            dma((3, n_emb)),
            dma((3, n_emb)),
            dma((9 * n_emb,)),
            dma((n_seq, n_emb, 2)),
            dma((ITERS + 1,)),
            dma((ITERS + 1,)),
            dma((ITERS, 2 * n_seq)),
            dma((ITERS, 2 * n_seq)),
            dma((n_emb,)),
            dma((n_emb,)),
        ],
        compiler_params=pltpu.CompilerParams(
            collective_id=0, has_side_effects=True, vmem_limit_bytes=48 << 20
        ),
        name="fused_sinkhorn",
    )(source, target, offs, sdoc, tdoc)
    row_mass = lax.dynamic_slice_in_dim(mass[0], (e % 2) * (rows // 2), rows // 2, 0)
    return projected, row_mass


def solution(mesh):
    in_specs = (P("seq", "emb"), P("seq", "emb"), P(), P(("seq", "emb")))
    out_specs = (P("seq", "emb"), P(("seq", "emb")))

    def whole(source, target, doc_ids, offsets):
        n_seq, n_emb = mesh.shape["seq"], mesh.shape["emb"]
        fits = (n_seq, n_emb) == (8, 4) and source.shape == (8192, 1024)
        body = fused_device if fits else per_device
        return jax.shard_map(
            body, mesh=mesh, in_specs=in_specs, out_specs=out_specs, check_vma=False
        )(source, target, doc_ids, offsets)

    return whole
```

```python
import functools

import jax
import jax.numpy as jnp
from jax import lax
from jax.experimental import pallas as pl
from jax.experimental.pallas import tpu as pltpu
from jax.sharding import PartitionSpec as P

BAND = 2048
OFFSET_BLOCK = 64
ITERS = 3


INV_EPS = 50.0
PENALTY = 0.04


def shifted_2(block, axis, distance):
    devices = range(lax.axis_size(axis))
    route = [(i - distance, i) for i in devices if i - distance in devices]
    return lax.ppermute(block, axis, route)


def per_device(source, target, doc_ids, offsets):
    n_emb = lax.axis_size("emb")
    rows_dev = source.shape[0] // n_emb
    place = lax.axis_index(("seq", "emb"))
    sentences = doc_ids.shape[0]
    reach = 2 * BAND
    hops = reach // rows_dev
    width = rows_dev + 2 * reach
    src_rows, tgt_rows = (
        lax.all_to_all(source, "emb", split_axis=0, concat_axis=1, tiled=True),
        lax.all_to_all(target, "emb", split_axis=0, concat_axis=1, tiled=True),
    )
    lower = {}
    upper = {}
    for dist in range(1, hops + 1):
        for sign in (1, -1):
            moved = shifted_2(tgt_rows, ("seq", "emb"), -sign * dist)
            if sign > 0:
                upper[dist] = moved
            else:
                lower[dist] = moved
    pieces = (
        [lower[dist] for dist in range(hops, 0, -1)]
        + [tgt_rows]
        + [upper[dist] for dist in range(1, hops + 1)]
    )
    window = jnp.concatenate(pieces, axis=0)
    src_scale = lax.rsqrt(jnp.sum(jnp.square(src_rows.astype(jnp.float32)), axis=1) + 1e-06)
    tgt_scale = lax.rsqrt(jnp.sum(jnp.square(window.astype(jnp.float32)), axis=1) + 1e-06)
    first_row = place * rows_dev
    src_pos = first_row + jnp.arange(rows_dev, dtype=jnp.int32)
    tgt_pos = first_row - reach + jnp.arange(width, dtype=jnp.int32)
    valid = (tgt_pos >= 0) & (tgt_pos < sentences)
    shifted = jnp.repeat(offsets, OFFSET_BLOCK)
    band = (jnp.abs(tgt_pos[None, :] - src_pos[:, None] - shifted[:, None]) <= BAND) & valid[
        None, :
    ]
    pad_docs = jnp.pad(doc_ids, (reach, reach), constant_values=-1)
    same = (
        lax.dynamic_slice_in_dim(doc_ids, first_row, rows_dev, 0)[:, None]
        == lax.dynamic_slice_in_dim(pad_docs, first_row, width, 0)[None, :]
    )
    penalty = jnp.where(same, 0.0, PENALTY)

    def cosines():
        dots = lax.dot_general(
            src_rows, window, (((1,), (1,)), ((), ())), preferred_element_type=jnp.float32
        )
        return dots * src_scale[:, None] * tgt_scale[None, :]

    def to_kernel(cosine):
        return jnp.where(band, jnp.exp((cosine - penalty) * INV_EPS), 0.0)

    def kernel():
        return to_kernel(cosines())

    scaling = valid.astype(jnp.float32)
    inverse = jnp.zeros((rows_dev,), jnp.float32)
    for step in range(ITERS):
        kern = kernel()
        inverse = 1.0 / jnp.sum(kern * scaling[None, :], axis=1)
        part = jnp.sum(kern * inverse[:, None], axis=0)
        owned = part[reach : reach + rows_dev]
        for lag in range(-hops, hops + 1):
            if lag != 0:
                begin = reach + lag * rows_dev
                owned = owned + shifted_2(part[begin : begin + rows_dev], ("seq", "emb"), lag)
        own_scaling = 1.0 / owned
        parts_list = []
        for lag in range(-hops, hops + 1):
            if lag == 0:
                parts_list.append(own_scaling)
            else:
                parts_list.append(shifted_2(own_scaling, ("seq", "emb"), -lag))
        scaling = jnp.concatenate(parts_list, axis=0)
    kern = kernel()
    totals = jnp.sum(kern * scaling[None, :], axis=1)
    row_mass = inverse * totals
    weights = (kern * scaling[None, :] / totals[:, None]).astype(jnp.bfloat16)
    mixed = jnp.dot(weights, window, preferred_element_type=jnp.float32).astype(jnp.bfloat16)
    projected = lax.all_to_all(mixed, "emb", split_axis=1, concat_axis=0, tiled=True)
    return (projected, row_mass)


F32 = jnp.float32
BF16 = jnp.bfloat16
MESH = pl.DeviceIdType.MESH


def flip(value, mask):
    for bit in (1, 2, 4):
        if mask & bit:
            value = value + bit * (1 - 2 * ((value // bit) % 2))
    return value


def fused_kernel(
    src_in, tgt_in, offs_in, sdoc, tdoc, out, mass,
    src_all, tgt_all, offs, kmat, wmat, sscale, tscale, rowacc, rowbuf, invcol, invrow, scal, colpart, tsq,
    colbuf, piece, pieces_in, z_ssem, z_rsem, t_ssem, t_rsem, row_ssem, row_rsem, col_ssem, col_rsem,
    p_ssem, p_rsem,
):
    n_seq, n_emb = lax.axis_size("seq"), lax.axis_size("emb")
    s, e = lax.axis_index("seq"), lax.axis_index("emb")
    eh, el = e // 2, e % 2
    block, feats = src_in.shape
    rows = src_all.shape[0]
    held = block // 2
    half = held // 2

    def remote(src, dst, ssem, rsem, seq, emb):
        return pltpu.make_async_remote_copy(
            src_ref=src, dst_ref=dst, send_sem=ssem, recv_sem=rsem,
            device_id=(seq, emb), device_id_type=MESH,
        )

    barrier = pltpu.get_barrier_semaphore()
    met = [(0, 1), (0, 2), (0, 3), (1, 0), (2, 0), (4, 0), (6, 0), (1, 2)]
    for k, j in met:
        pl.semaphore_signal(
            barrier, inc=1, device_id=(flip(s, k), flip(e, j)), device_id_type=MESH
        )
    pl.semaphore_wait(barrier, len(met))

    def cols(f):
        return pl.ds(pl.multiple_of(f * feats, feats), feats)

    def region(slot, j, start=0, count=held):
        return tgt_all.at[pl.ds(pl.multiple_of(slot * held + start, half), count), cols(flip(e, j))]

    sent = []

    def start(copy):
        copy.start()
        sent.append(copy)

    mine_t = pl.ds(pl.multiple_of(s * held, held), held)
    inner = ((e + 1) // 2) % 2

    def src_part(part):
        return src_in.at[pl.ds(pl.multiple_of(part * rows, rows), rows), :]

    start(remote(
        src_part(1 - eh), src_all.at[:, cols(e)], z_ssem.at[1, 2], z_rsem.at[1, 2 + inner], s, 2 - eh,
    ))
    for j in range(1, n_emb):
        peer = flip(e, j)
        start(remote(
            tgt_in.at[pl.ds(pl.multiple_of((peer % 2) * held, held), held), :],
            tgt_all.at[mine_t, cols(e)], z_ssem.at[0, j], z_rsem.at[0, j], s, peer,
        ))
    start(remote(
        src_part(eh), src_all.at[:, cols(e)], z_ssem.at[1, 1], z_rsem.at[1, 1], s, flip(e, 1),
    ))
    start(remote(offs_in, offs.at[el], z_ssem.at[2, 0], z_rsem.at[2, 0], s, flip(e, 1)))
    tgt_all[mine_t, cols(e)] = tgt_in[pl.ds(pl.multiple_of(el * held, held), held), :]
    src_all[:, cols(e)] = src_in[pl.ds(pl.multiple_of(eh * rows, rows), rows), :]
    offs[el] = offs_in[...]

    def src_arrived(j):
        at = src_all.at[:, cols(flip(e, j))]
        remote(at, at, z_ssem.at[1, 0], z_rsem.at[1, j], s, e).wait_recv()

    def handed_on(j):
        at = src_all.at[:, cols(flip(e, j))]
        return remote(at, at, z_ssem.at[2, j], z_rsem.at[1, 5 - j], s, flip(e, 1))

    count = [0]

    def send(slot, j, k, to, begin=0, length=held, part=0):
        at = region(slot, j, begin, length)
        start(remote(at, at, t_ssem.at[count[0]], t_rsem.at[k, j, part], flip(s, to), e))
        count[0] += 1

    def arrived(k, j, begin=0, length=held, part=0):
        at = region(flip(s, k), j, begin, length)
        remote(at, at, t_ssem.at[0], t_rsem.at[k, j, part], s, e).wait_recv()

    def first(j):
        if j:
            at = region(s, j)
            remote(at, at, z_ssem.at[0, 0], z_rsem.at[0, j], s, e).wait_recv()
        send(s, j, 2, 2)
        send(s, j, 4, 4)
        send(s, j, 1, 1)

    def second(j):
        arrived(2, j)
        send(flip(s, 2), j, 6, 4, 0, half, 0)
        send(flip(s, 2), j, 3, 1)
        arrived(4, j)
        send(flip(s, 4), j, 6, 2, half, half, 1)
        send(flip(s, 4), j, 5, 1)

    def third(j):
        for part in range(2):
            arrived(6, j, part * half, half, part)
            send(flip(s, 6), j, 7, 1, part * half, half, part)

    lanes = 128
    depth = src_all.shape[1]

    def fourth(j):
        for k in (1, 3, 5):
            arrived(k, j)
        for part in range(2):
            arrived(7, j, part * half, half, part)
        if j == 1:
            src_arrived(1)
        elif j:
            @pl.when(inner == 0)
            def _():
                src_arrived(j)

        f = flip(e, j)

        def squares(ref, at):
            acc = None
            for c in range(feats // lanes):
                ct = pl.ds(pl.multiple_of(f * feats + c * lanes, lanes), lanes)
                x = ref[at, ct].astype(F32)
                acc = x * x if acc is None else acc + x * x
            return acc

        @pl.loop(0, rows // 64)
        def _(r):
            at = pl.ds(pl.multiple_of(r * 64, 64), 64)
            total = squares(src_all, at)
            if j:
                total = total + sscale[at, :]
            if j == n_emb - 1:
                total = jnp.sum(total, axis=1, keepdims=True)
                total = jnp.broadcast_to(lax.rsqrt(total + 1e-6), (64, lanes))
            sscale[at, :] = total

        @pl.loop(0, n_seq)
        def _(slot):
            base = slot * held
            at = pl.ds(pl.multiple_of(base, held), held)

            @pl.loop(0, rows // 256)
            def _(r):
                rt = pl.ds(pl.multiple_of(r * 256, 256), 256)
                dots = lax.dot_general(
                    src_all[rt, cols(f)], tgt_all[at, cols(f)], (((1,), (1,)), ((), ())),
                    preferred_element_type=F32,
                )
                kmat[rt, at] = kmat[rt, at] + dots if j else dots

            for c in range(held // lanes):
                tt = pl.ds(pl.multiple_of(base + c * lanes, lanes), lanes)
                acc = squares(tgt_all, tt)
                if j:
                    acc = acc + tsq[tt, :]
                if j < n_emb - 1:
                    tsq[tt, :] = acc
                else:
                    total = jnp.sum(jnp.transpose(acc), axis=0, keepdims=True)
                    tscale[slot, :, pl.ds(c * lanes, lanes)] = jnp.broadcast_to(
                        lax.rsqrt(total + 1e-6), (8, lanes)
                    )

    first(0)

    @pl.when(inner == 1)
    def _():
        for j in (2, 3):
            src_arrived(j)
            handed_on(j).start()

    for j in range(1, n_emb + 1):
        if j < n_emb:
            first(j)
        second(j - 1)
        third(j - 1)
        fourth(j - 1)

    at = offs.at[1 - el]
    remote(at, at, z_ssem.at[2, 0], z_rsem.at[2, 0], s, e).wait_recv()

    per_part = offs_in.shape[0]

    @pl.loop(0, rows // OFFSET_BLOCK)
    def _(r):
        at = pl.ds(pl.multiple_of(r * OFFSET_BLOCK, OFFSET_BLOCK), OFFSET_BLOCK)
        shift = offs[r // per_part, r % per_part, 0:1, :]
        pos = (
            s * block + eh * rows + r * OFFSET_BLOCK
            + lax.broadcasted_iota(jnp.int32, (OFFSET_BLOCK, lanes), 0) + shift
        )
        docs = sdoc[at, :]
        scale = sscale[at, :]
        acc = jnp.zeros((OFFSET_BLOCK, lanes), F32)

        def one(slot, acc):
            for c in range(held // lanes):
                ct = pl.ds(pl.multiple_of(slot * held + c * lanes, lanes), lanes)
                cl = pl.ds(c * lanes, lanes)
                tpos = (
                    slot * block + el * held + c * lanes
                    + lax.broadcasted_iota(jnp.int32, (1, lanes), 1)
                )
                cosine = kmat[at, ct] * scale * tscale[slot, 0:1, cl]
                penalty = jnp.where(docs == tdoc[slot, 0:1, cl], 0.0, PENALTY)
                value = jnp.exp((cosine - penalty) * INV_EPS)
                value = jnp.where(jnp.abs(tpos - pos) <= BAND, value, 0.0)
                kmat[at, ct] = value
                acc = acc + value
            return acc

        rowacc[at, :] = lax.fori_loop(0, n_seq, one, acc)

    def row_start(step):
        turned = jnp.transpose(rowacc[...])
        part = turned[0:8]
        for g in range(1, lanes // 8):
            part = part + turned[8 * g : 8 * g + 8]
        rowbuf[step, 0] = part
        copy = remote(
            rowbuf.at[step, 0], rowbuf.at[step, 1], row_ssem.at[step], row_rsem.at[step],
            s, flip(e, 1),
        )
        copy.start()
        return copy

    def row_finish(step, copy):
        copy.wait()
        return jnp.sum(rowbuf[step, 0] + rowbuf[step, 1], axis=0, keepdims=True)

    def exchange(step, level, value, route):
        colbuf[step, level, 0] = value
        copies = []
        for p, (k, j) in enumerate(route, 1):
            copies.append(remote(
                colbuf.at[step, level, 0], colbuf.at[step, level, p],
                col_ssem.at[step, level, p], col_rsem.at[step, level, p], flip(s, k), flip(e, j),
            ))
            copies[-1].start()
        total = value
        for p, copy in enumerate(copies, 1):
            copy.wait()
            total = total + colbuf[step, level, p]
        return total

    def iterate(step):
        inverse = 1.0 / row_finish(step, row_start(step))
        invrow[...] = jnp.broadcast_to(inverse, invrow.shape)
        invcol[...] = jnp.transpose(jnp.broadcast_to(inverse, (lanes, rows)))

        @pl.loop(0, n_seq)
        def _(slot):
            for c in range(held // lanes):
                ct = pl.ds(pl.multiple_of(slot * held + c * lanes, lanes), lanes)
                colpart[slot, :, pl.ds(c * lanes, lanes)] = jnp.sum(
                    (kmat[:, ct] * invcol[...]).reshape(rows // 8, 8, lanes), axis=0
                )

        for slot in range(n_seq):
            scal[slot : slot + 1, :] = jnp.sum(colpart[slot], axis=0, keepdims=True)
        total = exchange(step, 0, scal[...], [(1, 0), (0, 2), (1, 2)])
        scal[...] = 1.0 / exchange(step, 1, total, [(2, 0), (4, 0), (6, 0)])

    def row_sums(last):
        @pl.loop(0, rows // 64)
        def _(r):
            at = pl.ds(pl.multiple_of(r * 64, 64), 64)
            acc = jnp.zeros((64, lanes), F32)
            for slot in range(n_seq):
                for c in range(held // lanes):
                    ct = pl.ds(slot * held + c * lanes, lanes)
                    scaled = kmat[at, ct] * scal[slot : slot + 1, c * lanes : (c + 1) * lanes]
                    acc = acc + scaled
                    if last:
                        wmat[at, ct] = scaled.astype(BF16)
            rowacc[at, :] = acc

    @pl.loop(0, ITERS - 1)
    def _(step):
        iterate(step)
        row_sums(False)

    iterate(ITERS - 1)
    row_sums(True)

    totals_copy = row_start(ITERS)
    copies = []
    for j in (3, 2, 1, 0):
        f = flip(e, j)
        early = j == 3

        def product(rt):
            return jnp.dot(wmat[rt, :], tgt_all[:, cols(f)], preferred_element_type=F32)

        if early:
            @pl.loop(0, rows // 256)
            def _(r):
                rt = pl.ds(pl.multiple_of(r * 256, 256), 256)
                kmat[rt, 0:feats] = product(rt)

            totals = row_finish(ITERS, totals_copy)
            mass[...] = invrow[...] * totals
            invcol[...] = jnp.transpose(jnp.broadcast_to(1.0 / totals, (lanes, rows)))

        @pl.loop(0, rows // 256)
        def _(r):
            rt = pl.ds(pl.multiple_of(r * 256, 256), 256)
            mixed = kmat[rt, 0:feats] if early else product(rt)
            inv = invcol[rt, :]
            for c in range(feats // lanes):
                cl = slice(c * lanes, (c + 1) * lanes)
                piece[j, rt, cl] = (mixed[:, cl] * inv).astype(BF16)

        if j:
            copy = remote(piece.at[j], pieces_in.at[j], p_ssem.at[j], p_rsem.at[j], s, f)
            copy.start()
            copies.append(copy)
    for copy in copies:
        copy.wait_recv()
    mine = pl.ds(pl.multiple_of(eh * rows, rows), rows)
    other = pl.ds(pl.multiple_of((1 - eh) * rows, rows), rows)
    out[mine, :] = (piece[0].astype(F32) + pieces_in[1].astype(F32)).astype(BF16)
    out[other, :] = (pieces_in[2].astype(F32) + pieces_in[3].astype(F32)).astype(BF16)
    for copy in copies + sent:
        copy.wait_send()

    @pl.when(inner == 1)
    def _():
        for j in (2, 3):
            handed_on(j).wait_send()


def fused_device(source, target, doc_ids, offsets):
    n_seq, n_emb = lax.axis_size("seq"), lax.axis_size("emb")
    s, e = lax.axis_index("seq"), lax.axis_index("emb")
    block, feats = source.shape
    held = rows = block // 2
    depth = feats * n_emb
    width = n_seq * held
    tdoc = lax.dynamic_index_in_dim(doc_ids.reshape(n_seq, 2, held), e % 2, 1, keepdims=False)
    sdoc = lax.dynamic_slice_in_dim(doc_ids, s * block + (e // 2) * rows, rows, 0)
    sdoc = jnp.broadcast_to(sdoc[:, None], (rows, 128))
    tdoc = jnp.broadcast_to(tdoc[:, None], (n_seq, 8, held))
    offs = jnp.broadcast_to(offsets[:, None, None], (offsets.shape[0], 8, 128))
    vmem = pl.BlockSpec(memory_space=pltpu.VMEM)
    dma = pltpu.SemaphoreType.DMA
    projected, mass = pl.pallas_call(
        fused_kernel,
        out_shape=(
            jax.ShapeDtypeStruct((block, feats), BF16),
            jax.ShapeDtypeStruct((8, rows), F32),
        ),
        in_specs=[vmem] * 5,
        out_specs=(vmem, vmem),
        scratch_shapes=[
            pltpu.VMEM((rows, depth), BF16),
            pltpu.VMEM((width, depth), BF16),
            pltpu.VMEM((2, offsets.shape[0], 8, 128), jnp.int32),
            pltpu.VMEM((rows, width), F32),
            pltpu.VMEM((rows, width), BF16),
            pltpu.VMEM((rows, 128), F32),
            pltpu.VMEM((n_seq, 8, held), F32),
            pltpu.VMEM((rows, 128), F32),
            pltpu.VMEM((ITERS + 1, 2, 8, rows), F32),
            pltpu.VMEM((rows, 128), F32),
            pltpu.VMEM((8, rows), F32),
            pltpu.VMEM((n_seq, held), F32),
            pltpu.VMEM((n_seq, 8, held), F32),
            pltpu.VMEM((width, 128), F32),
            pltpu.VMEM((ITERS, 2, 4, n_seq, held), F32),
            pltpu.VMEM((n_emb, rows, feats), BF16),
            pltpu.VMEM((n_emb, rows, feats), BF16),
            dma((3, n_emb)),
            dma((3, n_emb)),
            dma((9 * n_emb,)),
            dma((n_seq, n_emb, 2)),
            dma((ITERS + 1,)),
            dma((ITERS + 1,)),
            dma((ITERS, 2, 4)),
            dma((ITERS, 2, 4)),
            dma((n_emb,)),
            dma((n_emb,)),
        ],
        compiler_params=pltpu.CompilerParams(
            collective_id=0, has_side_effects=True, vmem_limit_bytes=48 << 20
        ),
        name="fused_sinkhorn",
    )(source, target, offs, sdoc, tdoc)
    row_mass = lax.dynamic_slice_in_dim(mass[0], (e % 2) * (rows // 2), rows // 2, 0)
    return projected, row_mass


def solution(mesh):
    in_specs = (P("seq", "emb"), P("seq", "emb"), P(), P(("seq", "emb")))
    out_specs = (P("seq", "emb"), P(("seq", "emb")))

    def whole(source, target, doc_ids, offsets):
        n_seq, n_emb = mesh.shape["seq"], mesh.shape["emb"]
        fits = (n_seq, n_emb) == (8, 4) and source.shape == (8192, 1024)
        body = fused_device if fits else per_device
        return jax.shard_map(
            body, mesh=mesh, in_specs=in_specs, out_specs=out_specs, check_vma=False
        )(source, target, doc_ids, offsets)

    return whole
```

```python
import functools

import jax
import jax.numpy as jnp
from jax import lax
from jax.experimental import pallas as pl
from jax.experimental.pallas import tpu as pltpu
from jax.sharding import PartitionSpec as P

BAND = 2048
OFFSET_BLOCK = 64
ITERS = 3


INV_EPS = 50.0
PENALTY = 0.04


def shifted_2(block, axis, distance):
    devices = range(lax.axis_size(axis))
    route = [(i - distance, i) for i in devices if i - distance in devices]
    return lax.ppermute(block, axis, route)


def per_device(source, target, doc_ids, offsets):
    n_emb = lax.axis_size("emb")
    rows_dev = source.shape[0] // n_emb
    place = lax.axis_index(("seq", "emb"))
    sentences = doc_ids.shape[0]
    reach = 2 * BAND
    hops = reach // rows_dev
    width = rows_dev + 2 * reach
    src_rows, tgt_rows = (
        lax.all_to_all(source, "emb", split_axis=0, concat_axis=1, tiled=True),
        lax.all_to_all(target, "emb", split_axis=0, concat_axis=1, tiled=True),
    )
    lower = {}
    upper = {}
    for dist in range(1, hops + 1):
        for sign in (1, -1):
            moved = shifted_2(tgt_rows, ("seq", "emb"), -sign * dist)
            if sign > 0:
                upper[dist] = moved
            else:
                lower[dist] = moved
    pieces = (
        [lower[dist] for dist in range(hops, 0, -1)]
        + [tgt_rows]
        + [upper[dist] for dist in range(1, hops + 1)]
    )
    window = jnp.concatenate(pieces, axis=0)
    src_scale = lax.rsqrt(jnp.sum(jnp.square(src_rows.astype(jnp.float32)), axis=1) + 1e-06)
    tgt_scale = lax.rsqrt(jnp.sum(jnp.square(window.astype(jnp.float32)), axis=1) + 1e-06)
    first_row = place * rows_dev
    src_pos = first_row + jnp.arange(rows_dev, dtype=jnp.int32)
    tgt_pos = first_row - reach + jnp.arange(width, dtype=jnp.int32)
    valid = (tgt_pos >= 0) & (tgt_pos < sentences)
    shifted = jnp.repeat(offsets, OFFSET_BLOCK)
    band = (jnp.abs(tgt_pos[None, :] - src_pos[:, None] - shifted[:, None]) <= BAND) & valid[
        None, :
    ]
    pad_docs = jnp.pad(doc_ids, (reach, reach), constant_values=-1)
    same = (
        lax.dynamic_slice_in_dim(doc_ids, first_row, rows_dev, 0)[:, None]
        == lax.dynamic_slice_in_dim(pad_docs, first_row, width, 0)[None, :]
    )
    penalty = jnp.where(same, 0.0, PENALTY)

    def cosines():
        dots = lax.dot_general(
            src_rows, window, (((1,), (1,)), ((), ())), preferred_element_type=jnp.float32
        )
        return dots * src_scale[:, None] * tgt_scale[None, :]

    def to_kernel(cosine):
        return jnp.where(band, jnp.exp((cosine - penalty) * INV_EPS), 0.0)

    def kernel():
        return to_kernel(cosines())

    scaling = valid.astype(jnp.float32)
    inverse = jnp.zeros((rows_dev,), jnp.float32)
    for step in range(ITERS):
        kern = kernel()
        inverse = 1.0 / jnp.sum(kern * scaling[None, :], axis=1)
        part = jnp.sum(kern * inverse[:, None], axis=0)
        owned = part[reach : reach + rows_dev]
        for lag in range(-hops, hops + 1):
            if lag != 0:
                begin = reach + lag * rows_dev
                owned = owned + shifted_2(part[begin : begin + rows_dev], ("seq", "emb"), lag)
        own_scaling = 1.0 / owned
        parts_list = []
        for lag in range(-hops, hops + 1):
            if lag == 0:
                parts_list.append(own_scaling)
            else:
                parts_list.append(shifted_2(own_scaling, ("seq", "emb"), -lag))
        scaling = jnp.concatenate(parts_list, axis=0)
    kern = kernel()
    totals = jnp.sum(kern * scaling[None, :], axis=1)
    row_mass = inverse * totals
    weights = (kern * scaling[None, :] / totals[:, None]).astype(jnp.bfloat16)
    mixed = jnp.dot(weights, window, preferred_element_type=jnp.float32).astype(jnp.bfloat16)
    projected = lax.all_to_all(mixed, "emb", split_axis=1, concat_axis=0, tiled=True)
    return (projected, row_mass)


F32 = jnp.float32
BF16 = jnp.bfloat16
MESH = pl.DeviceIdType.MESH


def flip(value, mask):
    for bit in (1, 2, 4):
        if mask & bit:
            value = value + bit * (1 - 2 * ((value // bit) % 2))
    return value


def fused_kernel(
    src_in, tgt_in, offs_in, sdoc, tdoc, out, mass,
    src_all, tgt_all, offs, kmat, wmat, sscale, tscale, rowacc, rowbuf, invcol, invrow, scal, colpart,
    colbuf, piece, pieces_in, z_ssem, z_rsem, t_ssem, t_rsem, row_ssem, row_rsem, col_ssem, col_rsem,
    p_ssem, p_rsem,
):
    n_seq, n_emb = lax.axis_size("seq"), lax.axis_size("emb")
    s, e = lax.axis_index("seq"), lax.axis_index("emb")
    eh, el = e // 2, e % 2
    block, feats = src_in.shape
    rows = src_all.shape[1]
    held = block // 2
    half = held // 2

    def remote(src, dst, ssem, rsem, seq, emb):
        return pltpu.make_async_remote_copy(
            src_ref=src, dst_ref=dst, send_sem=ssem, recv_sem=rsem,
            device_id=(seq, emb), device_id_type=MESH,
        )

    barrier = pltpu.get_barrier_semaphore()
    met = [(0, 1), (0, 2), (0, 3), (1, 0), (2, 0), (4, 0), (6, 0), (1, 2)]
    for k, j in met:
        pl.semaphore_signal(
            barrier, inc=1, device_id=(flip(s, k), flip(e, j)), device_id_type=MESH
        )
    pl.semaphore_wait(barrier, len(met))

    def region(slot, j, start=0, count=held):
        return tgt_all.at[flip(e, j), pl.ds(pl.multiple_of(slot * held + start, half), count), :]

    sent = []

    def start(copy):
        copy.start()
        sent.append(copy)

    mine_t = pl.ds(pl.multiple_of(s * held, held), held)

    def src_part(part):
        return src_in.at[pl.ds(pl.multiple_of(part * rows, rows), rows), :]

    for j in range(1, n_emb):
        peer = flip(e, j)
        start(remote(
            tgt_in.at[pl.ds(pl.multiple_of((peer % 2) * held, held), held), :],
            tgt_all.at[e, mine_t, :], z_ssem.at[0, j], z_rsem.at[0, j], s, peer,
        ))
    for j in range(1, n_emb):
        peer = flip(e, j)
        start(remote(
            src_part(peer // 2), src_all.at[e], z_ssem.at[1, j], z_rsem.at[1, j], s, peer,
        ))
    start(remote(offs_in, offs.at[el], z_ssem.at[2, 0], z_rsem.at[2, 0], s, flip(e, 1)))
    tgt_all[e, mine_t, :] = tgt_in[pl.ds(pl.multiple_of(el * held, held), held), :]
    src_all[e] = src_in[pl.ds(pl.multiple_of(eh * rows, rows), rows), :]
    offs[el] = offs_in[...]

    def src_arrived(j):
        at = src_all.at[flip(e, j)]
        remote(at, at, z_ssem.at[1, 0], z_rsem.at[1, j], s, e).wait_recv()

    count = [0]

    def send(slot, j, k, to, begin=0, length=held, part=0):
        at = region(slot, j, begin, length)
        start(remote(at, at, t_ssem.at[count[0]], t_rsem.at[k, j, part], flip(s, to), e))
        count[0] += 1

    def arrived(k, j, begin=0, length=held, part=0):
        at = region(flip(s, k), j, begin, length)
        remote(at, at, t_ssem.at[0], t_rsem.at[k, j, part], s, e).wait_recv()

    def first(j):
        if j:
            at = region(s, j)
            remote(at, at, z_ssem.at[0, 0], z_rsem.at[0, j], s, e).wait_recv()
        send(s, j, 2, 2)
        send(s, j, 4, 4)
        send(s, j, 1, 1)

    def second(j):
        arrived(2, j)
        send(flip(s, 2), j, 6, 4, 0, half, 0)
        send(flip(s, 2), j, 3, 1)
        arrived(4, j)
        send(flip(s, 4), j, 6, 2, half, half, 1)
        send(flip(s, 4), j, 5, 1)

    def third(j):
        for part in range(2):
            arrived(6, j, part * half, half, part)
            send(flip(s, 6), j, 7, 1, part * half, half, part)

    lanes = 128

    for step in range(n_emb + 2):
        for stage, lag in ((first, 0), (second, 1), (third, 2)):
            if 0 <= step - lag < n_emb:
                stage(step - lag)

    def squares(ref, at):
        acc = jnp.zeros((at.size, lanes), F32)
        for f in range(n_emb):
            for c in range(feats // lanes):
                x = ref[f, at, pl.ds(c * lanes, lanes)].astype(F32)
                acc = acc + x * x
        return acc

    for j in range(n_emb):
        for k in (1, 3, 5):
            arrived(k, j)
        for part in range(2):
            arrived(7, j, part * half, half, part)

    @pl.loop(0, n_seq)
    def _(slot):
        @pl.loop(0, held // lanes)
        def _(c):
            tt = pl.ds(pl.multiple_of(slot * held + c * lanes, lanes), lanes)
            total = jnp.sum(jnp.transpose(squares(tgt_all, tt)), axis=0, keepdims=True)
            tscale[slot, :, pl.ds(pl.multiple_of(c * lanes, lanes), lanes)] = jnp.broadcast_to(
                lax.rsqrt(total + 1e-6), (8, lanes)
            )

    for j in range(1, n_emb):
        src_arrived(j)

    @pl.loop(0, rows // 64)
    def _(r):
        at = pl.ds(pl.multiple_of(r * 64, 64), 64)
        total = jnp.sum(squares(src_all, at), axis=1, keepdims=True)
        sscale[at, :] = jnp.broadcast_to(lax.rsqrt(total + 1e-6), (64, lanes))

    @pl.loop(0, n_seq)
    def _(slot):
        at = pl.ds(pl.multiple_of(slot * held, held), held)

        @pl.loop(0, rows // 256)
        def _(r):
            rt = pl.ds(pl.multiple_of(r * 256, 256), 256)
            dots = None
            for f in range(n_emb):
                dot = lax.dot_general(
                    src_all[f, rt, :], tgt_all[f, at, :], (((1,), (1,)), ((), ())),
                    preferred_element_type=F32,
                )
                dots = dot if dots is None else dots + dot
            kmat[rt, at] = dots

    at = offs.at[1 - el]
    remote(at, at, z_ssem.at[2, 0], z_rsem.at[2, 0], s, e).wait_recv()

    per_part = offs_in.shape[0]

    @pl.loop(0, rows // OFFSET_BLOCK)
    def _(r):
        at = pl.ds(pl.multiple_of(r * OFFSET_BLOCK, OFFSET_BLOCK), OFFSET_BLOCK)
        shift = offs[r // per_part, r % per_part, 0:1, :]
        pos = (
            s * block + eh * rows + r * OFFSET_BLOCK
            + lax.broadcasted_iota(jnp.int32, (OFFSET_BLOCK, lanes), 0) + shift
        )
        docs = sdoc[at, :]
        scale = sscale[at, :]
        acc = jnp.zeros((OFFSET_BLOCK, lanes), F32)

        def one(slot, acc):
            for c in range(held // lanes):
                ct = pl.ds(pl.multiple_of(slot * held + c * lanes, lanes), lanes)
                cl = pl.ds(c * lanes, lanes)
                tpos = (
                    slot * block + el * held + c * lanes
                    + lax.broadcasted_iota(jnp.int32, (1, lanes), 1)
                )
                cosine = kmat[at, ct] * scale * tscale[slot, 0:1, cl]
                penalty = jnp.where(docs == tdoc[slot, 0:1, cl], 0.0, PENALTY)
                value = jnp.exp((cosine - penalty) * INV_EPS)
                value = jnp.where(jnp.abs(tpos - pos) <= BAND, value, 0.0)
                kmat[at, ct] = value
                acc = acc + value
            return acc

        rowacc[at, :] = lax.fori_loop(0, n_seq, one, acc)

    def row_start(step):
        turned = jnp.transpose(rowacc[...])
        part = turned[0:8]
        for g in range(1, lanes // 8):
            part = part + turned[8 * g : 8 * g + 8]
        rowbuf[step, 0] = part
        copy = remote(
            rowbuf.at[step, 0], rowbuf.at[step, 1], row_ssem.at[step], row_rsem.at[step],
            s, flip(e, 1),
        )
        copy.start()
        return copy

    def row_finish(step, copy):
        copy.wait()
        return jnp.sum(rowbuf[step, 0] + rowbuf[step, 1], axis=0, keepdims=True)

    def exchange(step, level, value, route):
        colbuf[step, level, 0] = value
        copies = []
        for p, (k, j) in enumerate(route, 1):
            copies.append(remote(
                colbuf.at[step, level, 0], colbuf.at[step, level, p],
                col_ssem.at[step, level, p], col_rsem.at[step, level, p], flip(s, k), flip(e, j),
            ))
            copies[-1].start()
        total = value
        for p, copy in enumerate(copies, 1):
            copy.wait()
            total = total + colbuf[step, level, p]
        return total

    def iterate(step):
        inverse = 1.0 / row_finish(step, row_start(step))
        invrow[...] = jnp.broadcast_to(inverse, invrow.shape)
        invcol[...] = jnp.transpose(jnp.broadcast_to(inverse, (lanes, rows)))

        @pl.loop(0, n_seq)
        def _(slot):
            for c in range(held // lanes):
                ct = pl.ds(pl.multiple_of(slot * held + c * lanes, lanes), lanes)
                colpart[slot, :, pl.ds(c * lanes, lanes)] = jnp.sum(
                    (kmat[:, ct] * invcol[...]).reshape(rows // 8, 8, lanes), axis=0
                )

        for slot in range(n_seq):
            scal[slot : slot + 1, :] = jnp.sum(colpart[slot], axis=0, keepdims=True)
        total = exchange(step, 0, scal[...], [(1, 0), (0, 2), (1, 2)])
        scal[...] = 1.0 / exchange(step, 1, total, [(2, 0), (4, 0), (6, 0)])

    def row_sums(last):
        @pl.loop(0, rows // 64)
        def _(r):
            at = pl.ds(pl.multiple_of(r * 64, 64), 64)
            acc = jnp.zeros((64, lanes), F32)
            for slot in range(n_seq):
                for c in range(held // lanes):
                    ct = pl.ds(slot * held + c * lanes, lanes)
                    scaled = kmat[at, ct] * scal[slot : slot + 1, c * lanes : (c + 1) * lanes]
                    acc = acc + scaled
                    if last:
                        wmat[at, ct] = scaled.astype(BF16)
            rowacc[at, :] = acc

    @pl.loop(0, ITERS - 1)
    def _(step):
        iterate(step)
        row_sums(False)

    iterate(ITERS - 1)
    row_sums(True)

    totals_copy = row_start(ITERS)
    copies = []
    for j in (3, 2, 1, 0):
        f = flip(e, j)
        early = j == 3

        def product(rt):
            return jnp.dot(wmat[rt, :], tgt_all[f], preferred_element_type=F32)

        if early:
            @pl.loop(0, rows // 256)
            def _(r):
                rt = pl.ds(pl.multiple_of(r * 256, 256), 256)
                kmat[rt, 0:feats] = product(rt)

            totals = row_finish(ITERS, totals_copy)
            mass[...] = invrow[...] * totals
            invcol[...] = jnp.transpose(jnp.broadcast_to(1.0 / totals, (lanes, rows)))

        @pl.loop(0, rows // 256)
        def _(r):
            rt = pl.ds(pl.multiple_of(r * 256, 256), 256)
            mixed = kmat[rt, 0:feats] if early else product(rt)
            inv = invcol[rt, :]
            for c in range(feats // lanes):
                cl = slice(c * lanes, (c + 1) * lanes)
                piece[j, rt, cl] = (mixed[:, cl] * inv).astype(BF16)

        if j:
            copy = remote(piece.at[j], pieces_in.at[j], p_ssem.at[j], p_rsem.at[j], s, f)
            copy.start()
            copies.append(copy)
    for copy in copies:
        copy.wait_recv()
    mine = pl.ds(pl.multiple_of(eh * rows, rows), rows)
    other = pl.ds(pl.multiple_of((1 - eh) * rows, rows), rows)
    out[mine, :] = (piece[0].astype(F32) + pieces_in[1].astype(F32)).astype(BF16)
    out[other, :] = (pieces_in[2].astype(F32) + pieces_in[3].astype(F32)).astype(BF16)
    for copy in copies + sent:
        copy.wait_send()


def fused_device(source, target, doc_ids, offsets):
    n_seq, n_emb = lax.axis_size("seq"), lax.axis_size("emb")
    s, e = lax.axis_index("seq"), lax.axis_index("emb")
    block, feats = source.shape
    held = rows = block // 2
    width = n_seq * held
    tdoc = lax.dynamic_index_in_dim(doc_ids.reshape(n_seq, 2, held), e % 2, 1, keepdims=False)
    sdoc = lax.dynamic_slice_in_dim(doc_ids, s * block + (e // 2) * rows, rows, 0)
    sdoc = jnp.broadcast_to(sdoc[:, None], (rows, 128))
    tdoc = jnp.broadcast_to(tdoc[:, None], (n_seq, 8, held))
    offs = jnp.broadcast_to(offsets[:, None, None], (offsets.shape[0], 8, 128))
    vmem = pl.BlockSpec(memory_space=pltpu.VMEM)
    dma = pltpu.SemaphoreType.DMA
    projected, mass = pl.pallas_call(
        fused_kernel,
        out_shape=(
            jax.ShapeDtypeStruct((block, feats), BF16),
            jax.ShapeDtypeStruct((8, rows), F32),
        ),
        in_specs=[vmem] * 5,
        out_specs=(vmem, vmem),
        scratch_shapes=[
            pltpu.VMEM((n_emb, rows, feats), BF16),
            pltpu.VMEM((n_emb, width, feats), BF16),
            pltpu.VMEM((2, offsets.shape[0], 8, 128), jnp.int32),
            pltpu.VMEM((rows, width), F32),
            pltpu.VMEM((rows, width), BF16),
            pltpu.VMEM((rows, 128), F32),
            pltpu.VMEM((n_seq, 8, held), F32),
            pltpu.VMEM((rows, 128), F32),
            pltpu.VMEM((ITERS + 1, 2, 8, rows), F32),
            pltpu.VMEM((rows, 128), F32),
            pltpu.VMEM((8, rows), F32),
            pltpu.VMEM((n_seq, held), F32),
            pltpu.VMEM((n_seq, 8, held), F32),
            pltpu.VMEM((ITERS, 2, 4, n_seq, held), F32),
            pltpu.VMEM((n_emb, rows, feats), BF16),
            pltpu.VMEM((n_emb, rows, feats), BF16),
            dma((3, n_emb)),
            dma((3, n_emb)),
            dma((9 * n_emb,)),
            dma((n_seq, n_emb, 2)),
            dma((ITERS + 1,)),
            dma((ITERS + 1,)),
            dma((ITERS, 2, 4)),
            dma((ITERS, 2, 4)),
            dma((n_emb,)),
            dma((n_emb,)),
        ],
        compiler_params=pltpu.CompilerParams(
            collective_id=0, has_side_effects=True, vmem_limit_bytes=48 << 20
        ),
        name="fused_sinkhorn",
    )(source, target, offs, sdoc, tdoc)
    row_mass = lax.dynamic_slice_in_dim(mass[0], (e % 2) * (rows // 2), rows // 2, 0)
    return projected, row_mass


def solution(mesh):
    in_specs = (P("seq", "emb"), P("seq", "emb"), P(), P(("seq", "emb")))
    out_specs = (P("seq", "emb"), P(("seq", "emb")))

    def whole(source, target, doc_ids, offsets):
        n_seq, n_emb = mesh.shape["seq"], mesh.shape["emb"]
        fits = (n_seq, n_emb) == (8, 4) and source.shape == (8192, 1024)
        body = fused_device if fits else per_device
        return jax.shard_map(
            body, mesh=mesh, in_specs=in_specs, out_specs=out_specs, check_vma=False
        )(source, target, doc_ids, offsets)

    return whole
```
